256 devices in a mesh: row: 4 (over y), col: 64 (over x, z, core).
Axes of the slice: x: 4, y: 4, z: 8, core: 2. Of those that a mesh axis runs over, the one named last changes fastest.
Arguments:
- features_x: float32 [16384, 256], P('row'), may hold values from -6 to 6
- scale_x: float32 [16384], P('row'), may hold values from 0.3 to 9
- adjoint_x: float32 [16384], P('row'), may hold values from -6 to 6
- features_y: float32 [65536, 256], P('col'), may hold values from -6 to 6
- scale_y: float32 [65536], P('col'), may hold values from 0.3 to 9
- adjoint_y: float32 [65536], P('col'), may hold values from -6 to 6
Outputs:
- grad_x: float32 [16384, 256], P(('row', 'col'))
- grad_y: float32 [65536, 256], P('col', 'row')
The draws below stay inside these ranges and needn't reach their ends.
All inputs are finite; a program needn't handle non-finite values.
Results may differ from the reference program's by a relative error of at most 0.0003.
The reference program's roundings to bfloat16 on the way (of `weights`) count: a program that leaves them out, or rounds other values in their place, can miss the bound.
Values sent between devices are 32-bit elements; how exact they have to be, the bound alone decides.
A program may use at most 64 MiB of HBM per device.

```python
import math
import jax
import jax.numpy as jnp
from jax import lax

D = 256
SWEEPS = 2
N = 16384
M = 65536


def positions(count):
    return jnp.arange(count, dtype=jnp.float32) / float(max(count - 1, 1))


def draw_scale_x(key, part):
    key = jax.random.fold_in(key, 17)
    where = positions(N)
    noise = jnp.exp(jax.random.uniform(key, (N,), jnp.float32, math.log(0.3), math.log(1.5)))
    rise = jnp.exp(math.log(6.0) * where)
    return jnp.clip(noise * rise, 0.3, 9.0)


def draw_scale_y(key, part):
    key = jax.random.fold_in(key, 29)
    where = positions(M)
    noise = jnp.exp(jax.random.uniform(key, (M,), jnp.float32, math.log(0.3), math.log(1.5)))
    rise = jnp.exp(math.log(6.0) * where)
    return jnp.clip(noise * rise, 0.3, 9.0)


def level_of(key, shape, split, least, high):
    def one(dim, shards_of):
        draws = jax.random.uniform(jax.random.fold_in(jax.random.fold_in(key, 6), dim), (shards_of,), jnp.float32, least / len(split), high / len(split))
        return jnp.repeat(jnp.exp(draws), shape[dim] // shards_of).reshape((-1,) + (1,) * (len(shape) - dim - 1))

    level = one(*split[0])
    for cut in split[1:]:
        level = level * one(*cut)
    return level


def normal_values(key, extent, spread, most, cuts=(), held_as=jnp.bfloat16):
    array = spread * jax.random.normal(key, extent, jnp.float32)
    if cuts:
        array = array * level_of(key, extent, cuts, -0.22, 0.18)
    return jnp.clip(array, -most, most).astype(held_as)


def setup_inputs(seed: int = 0) -> dict:
    splits = jax.random.split(jax.random.key(seed), 7)
    features_x = normal_values(splits[0], (N, D), 1.0, 6.0, ((0, 4),), jnp.float32)
    scale_x = draw_scale_x(jax.random.fold_in(splits[6], 71), 0)
    adjoint_x = normal_values(splits[2], (N,), 1.0, 6.0, ((0, 4),), jnp.float32)
    features_y = normal_values(splits[3], (M, D), 1.0, 6.0, ((0, 64),), jnp.float32)
    scale_y = draw_scale_y(jax.random.fold_in(splits[6], 71), 0)
    adjoint_y = normal_values(splits[5], (M,), 1.0, 6.0, ((0, 64),), jnp.float32)
    return {"features_x": features_x, "scale_x": scale_x, "adjoint_x": adjoint_x, "features_y": features_y, "scale_y": scale_y, "adjoint_y": adjoint_y}


kernel_gain = 0.5

def plan_rows(rows_x, rows_u, cols_y, scale_y, factor):
    scores = lax.dot_general(rows_x, cols_y, (((1,), (1,)), ((), ())), preferred_element_type=jnp.float32)
    return rows_u[:, None] * jnp.exp(scores * factor) * scale_y[None, :]

def reference(features_x, scale_x, adjoint_x, features_y, scale_y, adjoint_y):
    width = features_x.shape[1]
    factor = kernel_gain / math.sqrt(width)
    xbf = features_x.astype(jnp.bfloat16)
    ybf = features_y.astype(jnp.bfloat16)
    total_rows = xbf.shape[0]
    block = min(512, total_rows)
    nblocks = total_rows // block
    xsplit = xbf.reshape(nblocks, block, width)
    usplit = scale_x.reshape(nblocks, block)
    hsplit = adjoint_x.reshape(nblocks, block)
    zero_cols = jnp.zeros((ybf.shape[0],), jnp.float32)

    def first(acc, item):
        plan = plan_rows(item[0], item[1], ybf, scale_y, factor)
        return (acc + lax.optimization_barrier(jnp.sum(plan, axis=0)), lax.optimization_barrier(jnp.sum(plan, axis=1)))
    col_tot, row_tot = lax.scan(first, zero_cols, (xsplit, usplit))
    tsplit = row_tot.reshape(nblocks, block)
    adj_row = adjoint_x
    adj_col = adjoint_y
    for turn_index in range(SWEEPS):
        current = adj_col

        def sweep_fn(acc, item):
            plan = plan_rows(item[0], item[1], ybf, scale_y, factor)
            fresh = item[2] - jnp.dot(plan, current, precision=lax.Precision.HIGHEST) / item[3]
            return (acc + jnp.dot(fresh, plan, precision=lax.Precision.HIGHEST), fresh)
        col_part, pieces = lax.scan(sweep_fn, zero_cols, (xsplit, usplit, hsplit, tsplit))
        adj_row = pieces.reshape(total_rows)
        adj_col = adjoint_y - col_part / col_tot
    asplit = adj_row.reshape(nblocks, block)
    final_col = adj_col

    def grad_fn(acc, item):
        plan = plan_rows(item[0], item[1], ybf, scale_y, factor)
        weights = (plan * (item[2][:, None] + final_col[None, :])).astype(jnp.bfloat16)
        rows_grad = factor * jnp.dot(weights, ybf, preferred_element_type=jnp.float32)
        cols_grad = lax.dot_general(weights, item[0], (((0,), (0,)), ((), ())), preferred_element_type=jnp.float32)
        return (acc + cols_grad, rows_grad)
    acc_y, pieces_x = lax.scan(grad_fn, jnp.zeros((ybf.shape[0], width), jnp.float32), (xsplit, usplit, asplit))
    grad_x = pieces_x.reshape(total_rows, width)
    grad_y = factor * acc_y
    return (grad_x, grad_y)
```

```python
import functools
import math

import jax
import jax.numpy as jnp
from jax import lax
from jax.experimental import pallas as pl
from jax.experimental.pallas import tpu as pltpu
from jax.sharding import PartitionSpec as P

KERNEL_GAIN = 0.5
WIDTH = 256
FACTOR = KERNEL_GAIN / math.sqrt(WIDTH)
L = 128
F32 = jnp.float32
BF16 = jnp.bfloat16
MESH = pl.DeviceIdType.MESH
NX, NY, NZ = 4, 4, 8
STRIP = 256
OTHERS_Z = (4, 3, 5, 2, 6, 1, 7)
OTHERS_4 = (2, 1, 3)
GROUP_YC = tuple((a, c) for a in (2, 1, 3, 0) for c in (0, 1) if (a, c) != (0, 0))


def kernel(
    sx_ref, ax_ref, sy_ref, ay_ref, x_hbm, y_hbm, gx_ref, gy_ref,
    xf, yf, xb, yb, xt, plan, wts, syv, ayv, rowb, ub, rt, mx, axd,
    vrow, xrow, zrow, vcol, crow, avec, ctot,
    ga, gb, a1, a2, az, bp, bm, bx, gy, gyc, y1, y2,
    in_sem, sem_s, sem_r,
):
    row = lax.axis_index("row")
    col = lax.axis_index("col")
    x = col // (NZ * 2)
    z = (col // 2) % NZ
    core = col % 2
    other = 1 - core

    def at(dy=0, dx=0, dz=0, dc=0):
        return (
            lax.rem(row + dy, NY),
            (lax.rem(x + dx, NX) * NZ + lax.rem(z + dz, NZ)) * 2 + lax.rem(core + dc, 2),
        )

    count = [0]
    sent = []

    def send(src, dst, device):
        n = count[0]
        count[0] += 1
        copy = pltpu.make_async_remote_copy(
            src_ref=src, dst_ref=dst, send_sem=sem_s.at[n], recv_sem=sem_r.at[n],
            device_id=device, device_id_type=MESH,
        )
        copy.start()
        sent.append(copy)
        return copy

    loads = [
        pltpu.make_async_copy(y_hbm, yf.at[core], in_sem.at[0]),
        pltpu.make_async_copy(x_hbm.at[0, :, core], xf.at[:, 0], in_sem.at[1]),
        pltpu.make_async_copy(x_hbm.at[1, :, core], xf.at[:, 1], in_sem.at[2]),
    ]
    for copy in loads:
        copy.start()

    barrier = pltpu.get_barrier_semaphore()
    peers = (
        [at(dz=d) for d in OTHERS_Z] + [at(dx=d) for d in OTHERS_4]
        + [at(dy=a, dc=c) for a, c in GROUP_YC]
    )
    for peer in peers:
        pl.semaphore_signal(barrier, inc=1, device_id=peer, device_id_type=MESH)

    lane = lax.broadcasted_iota(jnp.int32, (16, L), 1)
    first = core == 0

    def mine(ref):
        low, high = ref[0:16, :], ref[16:32, :]
        low_r, high_r = pltpu.roll(low, 64, 1), pltpu.roll(high, 64, 1)
        return jnp.where(lane < 64, jnp.where(first, low, low_r), jnp.where(first, high_r, high))

    def spread(vec, dst):
        for m in range(16):
            dst[m * L:(m + 1) * L, :] = jnp.broadcast_to(vec[m:m + 1, :], (L, L)).T

    def gather_rows(src, dst, which):
        for m in range(16):
            dst[which, m:m + 1, :] = jnp.sum(src[m * L:(m + 1) * L, :].T, axis=0, keepdims=True)

    axd[...] = mine(ax_ref)
    spread(mine(sx_ref), ub)
    syv[core] = sy_ref[...]
    ayv[core] = ay_ref[...]
    rt[...] = jnp.zeros_like(rt)
    mx[...] = jnp.zeros_like(mx)
    for copy in loads:
        copy.wait()

    def cast_x(i, _):
        xb[pl.ds(i * L, 64), :] = xf[i, 0].astype(BF16)
        xb[pl.ds(i * L + 64, 64), :] = xf[i, 1].astype(BF16)
        return 0
    lax.fori_loop(0, 16, cast_x, 0)

    def cast_y(half):
        def step(i, _):
            yb[half, pl.ds(i * L, L), :] = yf[half, pl.ds(i * L, L), :].astype(BF16)
            return 0
        lax.fori_loop(0, 8, step, 0)
    cast_y(core)

    def fold8(v):
        return jnp.sum(v.reshape(-1, 8, L), axis=0)

    def make_plan(half):
        def strip(i, cols):
            rows = pl.ds(pl.multiple_of(i * STRIP, STRIP), STRIP)
            out = []
            for j in range(2):
                s = lax.dot_general(
                    xb[rows, :], yb[half, j * 512:(j + 1) * 512, :],
                    (((1,), (1,)), ((), ())), preferred_element_type=F32,
                )
                u = ub[rows, :]
                acc_r = rt[rows, :]
                acc_m = mx[rows, :]
                for l in range(4):
                    t = j * 4 + l
                    p = (u * jnp.exp(s[:, l * L:(l + 1) * L] * FACTOR)) * syv[half, t:t + 1, :]
                    plan[half, rows, t * L:(t + 1) * L] = p
                    acc_r += p
                    acc_m += p * ayv[half, t:t + 1, :]
                    out.append(cols[t] + fold8(p))
                rt[rows, :] = acc_r
                mx[rows, :] = acc_m
            return tuple(out)
        cols = lax.fori_loop(0, 8, strip, tuple(jnp.zeros((8, L), F32) for _ in range(8)))
        for t in range(8):
            vcol[0, pl.ds(half * 8 + t, 1), :] = jnp.sum(cols[t], axis=0, keepdims=True)

    pl.semaphore_wait(barrier, len(peers))
    sib = at(dc=1)
    fetch = [
        send(y_hbm, yf.at[core], sib),
        send(sy_ref, syv.at[core], sib),
        send(ay_ref, ayv.at[core], sib),
    ]
    make_plan(core)
    for copy in fetch:
        copy.wait_recv()
    cast_y(other)
    make_plan(other)

    def reduce_rows(n):
        copies = [
            send(vrow.at[0:n], xrow.at[n - 1, k, 0:n], at(dx=d)) for k, d in enumerate(OTHERS_4)
        ]
        return copies

    def reduce_rows_z(n, copies):
        for copy in copies:
            copy.wait_recv()
        total = vrow[0:n]
        for k in range(3):
            total = total + xrow[n - 1, k, 0:n]
        vrow[2:2 + n] = total
        return [
            send(vrow.at[2:2 + n], zrow.at[n - 1, k, 0:n], at(dz=d)) for k, d in enumerate(OTHERS_Z)
        ]

    def finish_rows(n, copies):
        for copy in copies:
            copy.wait_recv()
        total = vrow[2:2 + n]
        for k in range(7):
            total = total + zrow[n - 1, k, 0:n]
        return total

    def drain():
        for copy in sent:
            copy.wait_send()
        sent.clear()

    def reduce_cols(n):
        src = vcol.at[2 - n:2]
        copies = [
            send(src, crow.at[n - 1, k, 0:n], at(dy=a, dc=c)) for k, (a, c) in enumerate(GROUP_YC)
        ]
        for copy in copies:
            copy.wait_recv()
        total = vcol[2 - n:2]
        for k in range(7):
            total = total + crow[n - 1, k, 0:n]
        return total

    gather_rows(rt, vrow, 0)
    gather_rows(mx, vrow, 1)
    copies = reduce_rows(2)

    def turn_x(i, _):
        rows = pl.ds(pl.multiple_of(i * L, L), L)
        xt[:, rows] = xb[rows, :].T
        return 0
    lax.fori_loop(0, 16, turn_x, 0)
    copies = reduce_rows_z(2, copies)
    total = finish_rows(2, copies)
    row_tot = total[0]
    adj_row = axd[...] - total[1] / row_tot
    spread(adj_row, rowb)

    def back():
        for half in range(2):
            def strip(i, cols):
                rows = pl.ds(pl.multiple_of(i * STRIP, STRIP), STRIP)
                r = rowb[rows, :]
                return tuple(
                    cols[t] + fold8(plan[half, rows, t * L:(t + 1) * L] * r) for t in range(8)
                )
            cols = lax.fori_loop(0, 8, strip, tuple(jnp.zeros((8, L), F32) for _ in range(8)))
            for t in range(8):
                vcol[1, half * 8 + t:half * 8 + t + 1, :] = jnp.sum(cols[t], axis=0, keepdims=True)

    back()
    total = reduce_cols(2)
    ay_all = ayv[...].reshape(16, L)
    col_tot = total[0]
    ctot[...] = col_tot
    avec[...] = ay_all - total[1] / col_tot
    drain()

    def mix(i, _):
        rows = pl.ds(pl.multiple_of(i * STRIP, STRIP), STRIP)
        acc = jnp.zeros((STRIP, L), F32)
        for half in range(2):
            for t in range(8):
                acc += plan[half, rows, t * L:(t + 1) * L] * avec[half * 8 + t:half * 8 + t + 1, :]
        mx[rows, :] = acc
        return 0
    lax.fori_loop(0, 8, mix, 0)
    gather_rows(mx, vrow, 0)
    copies = reduce_rows(1)
    copies = reduce_rows_z(1, copies)
    total = finish_rows(1, copies)
    adj_row = axd[...] - total[0] / row_tot
    spread(adj_row, rowb)
    back()
    total = reduce_cols(1)
    avec[...] = ay_all - total[0] / ctot[...]
    drain()

    def weigh(i, _):
        rows = pl.ds(pl.multiple_of(i * STRIP, STRIP), STRIP)
        r = rowb[rows, :]
        for half in range(2):
            for t in range(8):
                a = avec[half * 8 + t:half * 8 + t + 1, :]
                w = plan[half, rows, t * L:(t + 1) * L] * (r + a)
                wts[half, rows, t * L:(t + 1) * L] = w.astype(BF16)
        g = jnp.dot(wts[0, rows, :], yb[0], preferred_element_type=F32)
        g += jnp.dot(wts[1, rows, :], yb[1], preferred_element_type=F32)
        g = g * FACTOR
        xq = i // 4
        for mm in range(2):
            zq = lax.rem(2 * i + mm, 8)
            for h in range(2):
                piece = g[mm * L + h * 64:mm * L + h * 64 + 64, :]
                ga[2 * h + xq, zq] = piece[:, 0:L]
                gb[zq, 2 * h + xq] = piece[:, L:2 * L]
        return 0
    lax.fori_loop(0, 8, weigh, 0)

    def mod(v, n):
        return lax.rem(v, n)

    def ring_start(g, r1, r2, fwd, bwd, me):
        far, right, left = mod(me + 2, 4), mod(me + 1, 4), mod(me + 3, 4)
        one = [send(g.at[far, 0], r1.at[0], fwd), send(g.at[far, 1], r1.at[1], bwd)]
        two = [send(g.at[right, 1], r2.at[0, 1], fwd), send(g.at[left, 0], r2.at[1, 0], bwd)]
        return one, two

    def ring_middle(g, r1, r2, fwd, bwd, me, one, two):
        right, left = mod(me + 1, 4), mod(me + 3, 4)
        one[0].wait_recv()
        g[right, 0] = g[right, 0] + r1[0]
        two.append(send(g.at[right, 0], r2.at[0, 0], fwd))
        one[1].wait_recv()
        g[left, 1] = g[left, 1] + r1[1]
        two.append(send(g.at[left, 1], r2.at[1, 1], bwd))

    def ring_end(g, r2, me, two):
        for copy in two:
            copy.wait_recv()
        g[me] = g[me] + r2[0] + r2[1]

    ga_h = ga.reshape(4, 2, 4, 64, L)
    right_x, left_x = at(dx=1), at(dx=3)
    one_a, two_a = ring_start(ga_h, a1, a2, right_x, left_x, x)

    right_z, left_z = at(dz=1), at(dz=7)
    far = mod(z + 4, 8)
    fwd = [send(gb.at[far, 0:2], bp.at[0, 0:2], right_z)]
    bwd = [send(gb.at[far, 2:4], bm.at[0, 2:4], left_z)]

    def cols_of(half, dst):
        def step(n, _):
            cols = pl.ds(pl.multiple_of(n * 256, 256), 256)
            g = jnp.dot(xt[...], wts[half, :, cols], preferred_element_type=F32) * FACTOR
            for q in range(4):
                for h in range(2):
                    dst[q, h, :, cols] = g[q * 64 + h * 32:q * 64 + h * 32 + 32, :]
            return 0
        lax.fori_loop(0, 4, step, 0)

    cols_of(other, gyc.at[0])
    swap = send(gyc.at[0], gyc.at[1], sib)

    def z_step(s):
        ahead, behind = mod(z + 4 - s, 8), mod(z + 4 + s, 8)
        fwd[-1].wait_recv()
        if s == 1:
            gb[ahead, 0:2] = gb[ahead, 0:2] + bp[0, 0:2]
        else:
            gb[ahead] = gb[ahead] + bp[s - 1]
        fwd.append(send(gb.at[ahead], bp.at[s], right_z))
        bwd[-1].wait_recv()
        if s == 1:
            gb[behind, 2:4] = gb[behind, 2:4] + bm[0, 2:4]
        else:
            gb[behind] = gb[behind] + bm[s - 1]
        bwd.append(send(gb.at[behind], bm.at[s], left_z))

    z_step(1)
    cols_of(core, gy)
    ring_middle(ga_h, a1, a2, right_x, left_x, x, one_a, two_a)
    swap.wait_recv()
    gy[...] = gy[...] + gyc[1]
    right_y, left_y = at(dy=1), at(dy=3)
    one_y, two_y = ring_start(gy, y1, y2, right_y, left_y, row)
    z_step(2)
    ring_middle(gy, y1, y2, right_y, left_y, row, one_y, two_y)
    z_step(3)
    ring_end(ga_h, a2, x, two_a)
    last_a = [send(ga.at[x, mod(z + d, 8)], az.at[k], at(dz=d)) for k, d in enumerate(OTHERS_Z)]
    fwd[-1].wait_recv()
    bwd[-1].wait_recv()
    gb[z] = gb[z] + bp[3] + bm[3]
    last_b = [send(gb.at[z, mod(x + d, 4)], bx.at[k], at(dx=d)) for k, d in enumerate(OTHERS_4)]
    ring_end(gy, y2, row, two_y)
    gy_ref[0:32, :] = gy[row, 0]
    gy_ref[32:64, :] = gy[row, 1]
    total = gb[z, x]
    for k in range(3):
        last_b[k].wait_recv()
        total = total + bx[k]
    gx_ref[:, L:2 * L] = total
    total = ga[x, z]
    for k in range(7):
        last_a[k].wait_recv()
        total = total + az[k]
    gx_ref[:, 0:L] = total
    drain()


def body(features_x, scale_x, adjoint_x, features_y, scale_y, adjoint_y):
    vmem = pl.BlockSpec(memory_space=pltpu.VMEM)
    anym = pl.BlockSpec(memory_space=pl.ANY)
    V = pltpu.VMEM
    ncopies = 96
    gx, gy = pl.pallas_call(
        kernel,
        out_shape=(
            jax.ShapeDtypeStruct((64, WIDTH), F32),
            jax.ShapeDtypeStruct((64, 1024), F32),
        ),
        in_specs=[vmem, vmem, vmem, vmem, anym, anym],
        out_specs=(vmem, vmem),
        scratch_shapes=[
            V((16, 2, 64, WIDTH), F32), V((2, 1024, WIDTH), F32),
            V((2048, WIDTH), BF16), V((2, 1024, WIDTH), BF16), V((WIDTH, 2048), BF16),
            V((2, 2048, 1024), F32), V((2, 2048, 1024), BF16),
            V((2, 8, L), F32), V((2, 8, L), F32),
            V((2048, L), F32), V((2048, L), F32), V((2048, L), F32), V((2048, L), F32), V((16, L), F32),
            V((4, 16, L), F32), V((2, 3, 2, 16, L), F32), V((2, 7, 2, 16, L), F32),
            V((2, 16, L), F32), V((2, 7, 2, 16, L), F32), V((16, L), F32), V((16, L), F32),
            V((4, 8, 64, L), F32), V((8, 4, 64, L), F32),
            V((2, 4, 64, L), F32), V((2, 2, 4, 64, L), F32), V((7, 64, L), F32),
            V((4, 4, 64, L), F32), V((4, 4, 64, L), F32), V((3, 64, L), F32),
            V((4, 2, 32, 1024), F32), V((2, 4, 2, 32, 1024), F32),
            V((2, 32, 1024), F32), V((2, 2, 32, 1024), F32),
            pltpu.SemaphoreType.DMA((3,)),
            pltpu.SemaphoreType.DMA((ncopies,)), pltpu.SemaphoreType.DMA((ncopies,)),
        ],
        compiler_params=pltpu.CompilerParams(
            collective_id=0, has_side_effects=True, vmem_limit_bytes=60 * 2**20
        ),
        cost_estimate=pl.CostEstimate(
            flops=6 * 2048 * 2048 * 256, bytes_accessed=5 * 2**20, transcendentals=2048 * 2048
        ),
        name="sinkhorn_adjoint",
    )(
        scale_x.reshape(32, L), adjoint_x.reshape(32, L),
        scale_y.reshape(8, L), adjoint_y.reshape(8, L),
        features_x.reshape(2, 16, 2, 64, WIDTH), features_y,
    )
    return gx, gy.T


def solution(mesh):
    in_specs = (P("row", None), P("row"), P("row"), P("col", None), P("col"), P("col"))
    out_specs = (P(("row", "col"), None), P("col", "row"))
    return jax.shard_map(body, mesh=mesh, in_specs=in_specs, out_specs=out_specs, check_vma=False)
```

```python
import functools
import math

import jax
import jax.numpy as jnp
from jax import lax
from jax.experimental import pallas as pl
from jax.experimental.pallas import tpu as pltpu
from jax.sharding import PartitionSpec as P

KERNEL_GAIN = 0.5
WIDTH = 256
FACTOR = KERNEL_GAIN / math.sqrt(WIDTH)
L = 128
F32 = jnp.float32
BF16 = jnp.bfloat16
MESH = pl.DeviceIdType.MESH
NX, NY, NZ = 4, 4, 8
STRIP = 256
HALF = 1024
RA = 40
RB = 64 - RA
OTHERS_Z = (4, 3, 5, 2, 6, 1, 7)
OTHERS_4 = (2, 1, 3)
FAR_Z = (2, 1, 3, 0)
NEAR_Z = (4, 5, 7)
GROUP_YC = tuple((a, c) for a in (2, 1, 3, 0) for c in (0, 1) if (a, c) != (0, 0))


def kernel(
    sx_ref, ax_ref, sy_ref, ay_ref, x_hbm, y_hbm, gx_ref, gy_ref,
    xf, yf, xb, yb, xt, plan, wts, syv, ayv, rowb, ub, rt, mx, axd, colacc,
    vrow, xrow, zsrc, zrow, vcol, crow, vcol2, crow2, avec, rtot, ctot,
    ga, gb, a1, a2, az, b1, bp, bm, bx, gy, gyo, gyc, y1, y2,
    in_sem, sem_s, sem_r,
):
    row = lax.axis_index("row")
    col = lax.axis_index("col")
    x = col // (NZ * 2)
    z = (col // 2) % NZ
    core = col % 2
    other = 1 - core

    def at(dy=0, dx=0, dz=0, dc=0):
        return (
            lax.rem(row + dy, NY),
            (lax.rem(x + dx, NX) * NZ + lax.rem(z + dz, NZ)) * 2 + lax.rem(core + dc, 2),
        )

    count = [0]
    sent = []

    def send(src, dst, device):
        n = count[0]
        count[0] += 1
        copy = pltpu.make_async_remote_copy(
            src_ref=src, dst_ref=dst, send_sem=sem_s.at[n], recv_sem=sem_r.at[n],
            device_id=device, device_id_type=MESH,
        )
        copy.start()
        sent.append(copy)
        return copy

    def drain():
        for copy in sent:
            copy.wait_send()
        sent.clear()

    loads = [
        pltpu.make_async_copy(y_hbm, yf.at[core], in_sem.at[0]),
        pltpu.make_async_copy(x_hbm.at[0, :, core], xf.at[:, 0], in_sem.at[1]),
        pltpu.make_async_copy(x_hbm.at[1, :, core], xf.at[:, 1], in_sem.at[2]),
    ]
    for copy in loads:
        copy.start()

    barrier = pltpu.get_barrier_semaphore()
    peers = (
        [at(dz=d) for d in OTHERS_Z] + [at(dx=d) for d in OTHERS_4]
        + [at(dy=a, dc=c) for a, c in GROUP_YC]
    )
    for peer in peers:
        pl.semaphore_signal(barrier, inc=1, device_id=peer, device_id_type=MESH)

    lane = lax.broadcasted_iota(jnp.int32, (16, L), 1)
    first = core == 0

    def mine(ref):
        low, high = ref[0:16, :], ref[16:32, :]
        low_r, high_r = pltpu.roll(low, 64, 1), pltpu.roll(high, 64, 1)
        return jnp.where(lane < 64, jnp.where(first, low, low_r), jnp.where(first, high_r, high))

    def spread(vec, dst, start):
        for m in range(vec.shape[0]):
            here = start + m * L
            dst[here:here + L, :] = jnp.broadcast_to(vec[m:m + 1, :], (L, L)).T

    def gather_rows(src, chunk, dst):
        for m in range(8):
            here = chunk * HALF + m * L
            dst[m:m + 1, :] = jnp.sum(src[here:here + L, :].T, axis=0, keepdims=True)

    axd[...] = mine(ax_ref)
    spread(mine(sx_ref), ub, 0)
    syv[core] = sy_ref[...]
    ayv[core] = ay_ref[...]
    for copy in loads:
        copy.wait()

    def cast_x(i, _):
        xb[pl.ds(i * L, 64), :] = xf[i, 0].astype(BF16)
        xb[pl.ds(i * L + 64, 64), :] = xf[i, 1].astype(BF16)
        return 0
    lax.fori_loop(0, 16, cast_x, 0)

    def cast_y(half):
        def step(i, _):
            yb[half, pl.ds(i * L, L), :] = yf[half, pl.ds(i * L, L), :].astype(BF16)
            return 0
        lax.fori_loop(0, 8, step, 0)
    cast_y(core)

    def fold8(v):
        return jnp.sum(v.reshape(-1, 8, L), axis=0)

    def make_plan(half, i, fresh):
        rows = slice(i * HALF, (i + 1) * HALF)
        u = ub[rows, :]
        if fresh:
            acc_r = acc_m = None
        else:
            acc_r, acc_m = rt[rows, :], mx[rows, :]
        for j in range(4):
            s = lax.dot_general(
                xb[rows, :], yb[half, j * 256:(j + 1) * 256, :],
                (((1,), (1,)), ((), ())), preferred_element_type=F32,
            )
            for l in range(2):
                t = j * 2 + l
                p = (u * jnp.exp(s[:, l * L:(l + 1) * L] * FACTOR)) * syv[half, t:t + 1, :]
                plan[half, rows, t * L:(t + 1) * L] = p
                pa = p * ayv[half, t:t + 1, :]
                acc_r = p if acc_r is None else acc_r + p
                acc_m = pa if acc_m is None else acc_m + pa
                c = fold8(p)
                colacc[half, t] = c if i == 0 else colacc[half, t] + c
        rt[rows, :] = acc_r
        mx[rows, :] = acc_m

    sib = at(dc=1)
    make_plan(core, 0, True)
    pl.semaphore_wait(barrier, len(peers))
    fetch = [
        send(y_hbm, yf.at[core], sib),
        send(sy_ref, syv.at[core], sib),
        send(ay_ref, ayv.at[core], sib),
    ]
    make_plan(core, 1, True)
    for copy in fetch:
        copy.wait_recv()
    cast_y(other)

    def rows_x(k, n, c):
        return [
            send(vrow.at[k, c, 0:n], xrow.at[k, c, q, 0:n], at(dx=d))
            for q, d in enumerate(OTHERS_4)
        ]

    def rows_z(k, n, c, copies):
        for copy in copies:
            copy.wait_recv()
        total = vrow[k, c, 0:n]
        for q in range(3):
            total = total + xrow[k, c, q, 0:n]
        zsrc[k, c, 0:n] = total
        return [
            send(zsrc.at[k, c, 0:n], zrow.at[k, c, q, 0:n], at(dz=d))
            for q, d in enumerate(OTHERS_Z)
        ]

    def rows_end(k, n, c, copies):
        for copy in copies:
            copy.wait_recv()
        total = zsrc[k, c, 0:n]
        for q in range(7):
            total = total + zrow[k, c, q, 0:n]
        return total

    in_x = []
    for c in range(2):
        make_plan(other, c, False)
        gather_rows(rt, c, vrow.at[0, c, 0])
        gather_rows(mx, c, vrow.at[0, c, 1])
        in_x.append(rows_x(0, 2, c))
    in_z = [rows_z(0, 2, c, in_x[c]) for c in range(2)]
    for half in range(2):
        for t in range(8):
            vcol[0, half * 8 + t:half * 8 + t + 1, :] = jnp.sum(
                colacc[half, t], axis=0, keepdims=True)

    def turn_x(i, _):
        rows = pl.ds(pl.multiple_of(i * L, L), L)
        xt[:, rows] = xb[rows, :].T
        return 0
    lax.fori_loop(0, 16, turn_x, 0)

    def back(c):
        for half in range(2):
            def strip(i, cols):
                rows = pl.ds(pl.multiple_of(c * HALF + i * STRIP, STRIP), STRIP)
                r = rowb[rows, :]
                return tuple(
                    cols[t] + fold8(plan[half, rows, t * L:(t + 1) * L] * r) for t in range(8)
                )
            init = tuple(jnp.zeros((8, L), F32) if c == 0 else colacc[half, t] for t in range(8))
            cols = lax.fori_loop(0, HALF // STRIP, strip, init)
            for t in range(8):
                colacc[half, t] = cols[t]

    def back_end(dst):
        for half in range(2):
            for t in range(8):
                dst[half * 8 + t:half * 8 + t + 1, :] = jnp.sum(
                    colacc[half, t], axis=0, keepdims=True)

    def sum_cols(src, dst):
        copies = [
            send(src, dst.at[q], at(dy=a, dc=c)) for q, (a, c) in enumerate(GROUP_YC)
        ]
        for copy in copies:
            copy.wait_recv()
        total = src[...]
        for q in range(7):
            total = total + dst[q]
        return total

    for c in range(2):
        total = rows_end(0, 2, c, in_z[c])
        rtot[c * 8:(c + 1) * 8, :] = total[0]
        spread(axd[c * 8:(c + 1) * 8, :] - total[1] / total[0], rowb, c * HALF)
        back(c)
    back_end(vcol.at[1])
    total = sum_cols(vcol, crow)
    ay_all = ayv[...].reshape(16, L)
    ctot[...] = total[0]
    avec[...] = ay_all - total[1] / total[0]

    in_x = []
    for c in range(2):
        def mix(i, _):
            rows = pl.ds(pl.multiple_of(c * HALF + i * STRIP, STRIP), STRIP)
            acc = jnp.zeros((STRIP, L), F32)
            for half in range(2):
                for t in range(8):
                    acc += plan[half, rows, t * L:(t + 1) * L] * avec[half * 8 + t:half * 8 + t + 1, :]
            mx[rows, :] = acc
            return 0
        lax.fori_loop(0, HALF // STRIP, mix, 0)
        gather_rows(mx, c, vrow.at[1, c, 0])
        in_x.append(rows_x(1, 1, c))
    in_z = [rows_z(1, 1, c, in_x[c]) for c in range(2)]
    for c in range(2):
        total = rows_end(1, 1, c, in_z[c])
        spread(axd[c * 8:(c + 1) * 8, :] - total[0] / rtot[c * 8:(c + 1) * 8, :], rowb, c * HALF)
        back(c)
    back_end(vcol2)
    avec[...] = ay_all - sum_cols(vcol2, crow2) / ctot[...]

    par = lax.rem(x, 2)

    def weigh(order):
        side = par if order == 0 else 1 - par
        rows = pl.ds(pl.multiple_of(side * HALF, HALF), HALF)
        r = rowb[rows, :]
        for half in range(2):
            for t in range(8):
                a = avec[half * 8 + t:half * 8 + t + 1, :]
                w = plan[half, rows, t * L:(t + 1) * L] * (r + a)
                wts[half, rows, t * L:(t + 1) * L] = w.astype(BF16)
        g = jnp.dot(wts[0, rows, :], yb[0], preferred_element_type=F32)
        g += jnp.dot(wts[1, rows, :], yb[1], preferred_element_type=F32)
        g = g * FACTOR
        for m in range(8):
            off = lax.rem(m + 8 - z, 8)
            pos = lax.rem(off + 6, 8)
            for h in range(2):
                xo = lax.rem(2 * h + side + 4 - x, 4)
                piece = g[m * L + h * 64:m * L + h * 64 + 64, :]
                ga[xo, pos] = piece[0:RA, :]
                gb[off, order, xo // 2] = piece[RA:64, :]

    right_x, left_x = at(dx=1), at(dx=3)
    right_z, left_z = at(dz=1), at(dz=7)
    right_y, left_y = at(dy=1), at(dy=3)

    def lo(c):
        return slice(4 * c, 4 * c + 2)

    def hi(c):
        return slice(4 * c + 2, 4 * c + 4)

    weigh(0)
    one_a = [None, None]
    two_a = [[], []]
    for c in range(2):
        one_a[c] = (
            send(ga.at[2, lo(c)], a1.at[c, 0], right_x), send(ga.at[2, hi(c)], a1.at[c, 1], left_x)
        )
    one_b = [send(gb.at[4, 0], b1.at[0], right_z), None]
    fwd = [[None, None], [None, None], [None, None]]
    bwd = [[None, None], [None, None], [None, None]]
    bwd[0][0] = send(gb.at[5, 0], bm.at[0, 0], left_z)
    weigh(1)

    def a_direct(c):
        two_a[c].append(send(ga.at[1, hi(c)], a2.at[0, hi(c)], right_x))
        two_a[c].append(send(ga.at[3, lo(c)], a2.at[1, lo(c)], left_x))

    def a_summed(c):
        one_a[c][0].wait_recv()
        ga[1, lo(c)] = ga[1, lo(c)] + a1[c, 0]
        two_a[c].append(send(ga.at[1, lo(c)], a2.at[0, lo(c)], right_x))
        one_a[c][1].wait_recv()
        ga[3, hi(c)] = ga[3, hi(c)] + a1[c, 1]
        two_a[c].append(send(ga.at[3, hi(c)], a2.at[1, hi(c)], left_x))

    last_a = []

    def a_end(c):
        for copy in two_a[c]:
            copy.wait_recv()
        here = slice(4 * c, 4 * c + 4)
        ga[0, here] = ga[0, here] + a2[0, here] + a2[1, here]
        for p in FAR_Z if c == 0 else NEAR_Z:
            last_a.append(send(ga.at[0, p], az.at[len(last_a)], at(dz=(p + 2) % 8)))

    a_direct(0)
    one_b[1] = send(gb.at[4, 1], b1.at[1], left_z)
    fwd[0][1] = send(gb.at[3, 1], bp.at[0, 1], right_z)

    def cols_of(half, part, dst):
        g = jnp.dot(xt[...], wts[half, :, part * 512:(part + 1) * 512], preferred_element_type=F32)
        g = g * FACTOR
        for q in range(4):
            off = lax.rem(q + 4 - row, 4)
            for h in range(2):
                dst[part, off, h] = g[q * 64 + h * 32:q * 64 + h * 32 + 32, :]

    swap = []
    for part in range(2):
        cols_of(other, part, gyo)
        swap.append(send(gyo.at[part], gyc.at[part], sib))

    a_summed(0)
    a_direct(1)
    one_b[0].wait_recv()
    gb[3, 0] = gb[3, 0] + b1[0]
    fwd[0][0] = send(gb.at[3, 0], bp.at[0, 0], right_z)
    one_b[1].wait_recv()
    gb[5, 1] = gb[5, 1] + b1[1]
    bwd[0][1] = send(gb.at[5, 1], bm.at[0, 1], left_z)
    a_summed(1)

    one_y = [None, None]
    two_y = [[], []]

    def y_start(part):
        cols_of(core, part, gy)
        swap[part].wait_recv()
        gy[part] = gy[part] + gyc[part]
        one_y[part] = (
            send(gy.at[part, 2, 0], y1.at[part, 0], right_y),
            send(gy.at[part, 2, 1], y1.at[part, 1], left_y),
        )

    def y_direct(part):
        two_y[part].append(send(gy.at[part, 1, 1], y2.at[0, part, 1], right_y))
        two_y[part].append(send(gy.at[part, 3, 0], y2.at[1, part, 0], left_y))

    def y_summed(part):
        one_y[part][0].wait_recv()
        gy[part, 1, 0] = gy[part, 1, 0] + y1[part, 0]
        two_y[part].append(send(gy.at[part, 1, 0], y2.at[0, part, 0], right_y))
        one_y[part][1].wait_recv()
        gy[part, 3, 1] = gy[part, 3, 1] + y1[part, 1]
        two_y[part].append(send(gy.at[part, 3, 1], y2.at[1, part, 1], left_y))

    def y_end(part):
        for copy in two_y[part]:
            copy.wait_recv()
        for h in range(2):
            gy_ref[h * 32:(h + 1) * 32, part * 512:(part + 1) * 512] = (
                gy[part, 0, h] + y2[0, part, h] + y2[1, part, h]
            )

    def z_fwd(s, p):
        fwd[s - 3][p].wait_recv()
        gb[5 - s, p] = gb[5 - s, p] + bp[s - 3, p]
        fwd[s - 2][p] = send(gb.at[5 - s, p], bp.at[s - 2, p], right_z)

    def z_bwd(s, p):
        bwd[s - 3][p].wait_recv()
        gb[3 + s, p] = gb[3 + s, p] + bm[s - 3, p]
        bwd[s - 2][p] = send(gb.at[3 + s, p], bm.at[s - 2, p], left_z)

    last_b = []

    def b_end(p):
        fwd[2][p].wait_recv()
        bwd[2][p].wait_recv()
        gb[0, p] = gb[0, p] + bp[2, p] + bm[2, p]
        for h in range(2):
            if (h, p) != (0, 0):
                last_b.append(send(gb.at[0, p, h], bx.at[len(last_b)], at(dx=2 * h + p)))

    y_start(0)
    z_bwd(3, 0)
    z_fwd(3, 1)
    y_start(1)
    y_direct(0)
    z_fwd(3, 0)
    z_bwd(3, 1)
    y_direct(1)
    a_end(0)
    z_bwd(4, 0)
    z_fwd(4, 1)
    y_summed(0)
    a_end(1)
    z_fwd(4, 0)
    z_bwd(4, 1)
    y_summed(1)
    b_end(1)
    b_end(0)
    y_end(0)
    y_end(1)
    total = ga[0, 6]
    for q in range(7):
        last_a[q].wait_recv()
        total = total + az[q]
    gx_ref[0:RA, :] = total
    total = gb[0, 0, 0]
    for q in range(3):
        last_b[q].wait_recv()
        total = total + bx[q]
    gx_ref[RA:64, :] = total
    drain()


def finish(a_ref, b_ref, gx_ref, gy_ref):
    gx_ref[...] = a_ref[...]
    gy_ref[...] = b_ref[...]


def body(features_x, scale_x, adjoint_x, features_y, scale_y, adjoint_y):
    vmem = pl.BlockSpec(memory_space=pltpu.VMEM)
    anym = pl.BlockSpec(memory_space=pl.ANY)
    V = pltpu.VMEM
    ncopies = 107
    shapes = (
        jax.ShapeDtypeStruct((64, WIDTH), F32),
        jax.ShapeDtypeStruct((64, 1024), F32),
    )
    parts = pl.pallas_call(
        kernel,
        out_shape=shapes,
        in_specs=[vmem, vmem, vmem, vmem, anym, anym],
        out_specs=(vmem, vmem),
        scratch_shapes=[
            V((16, 2, 64, WIDTH), F32), V((2, 1024, WIDTH), F32),
            V((2048, WIDTH), BF16), V((2, 1024, WIDTH), BF16), V((WIDTH, 2048), BF16),
            V((2, 2048, 1024), F32), V((2, 2048, 1024), BF16),
            V((2, 8, L), F32), V((2, 8, L), F32),
            V((2048, L), F32), V((2048, L), F32), V((2048, L), F32), V((2048, L), F32),
            V((16, L), F32), V((2, 8, 8, L), F32),
            V((2, 2, 2, 8, L), F32), V((2, 2, 3, 2, 8, L), F32),
            V((2, 2, 2, 8, L), F32), V((2, 2, 7, 2, 8, L), F32),
            V((2, 16, L), F32), V((7, 2, 16, L), F32),
            V((16, L), F32), V((7, 16, L), F32), V((16, L), F32), V((16, L), F32), V((16, L), F32),
            V((4, 8, RA, WIDTH), F32), V((8, 2, 2, RB, WIDTH), F32),
            V((2, 2, 2, RA, WIDTH), F32), V((2, 8, RA, WIDTH), F32), V((7, RA, WIDTH), F32),
            V((2, 2, RB, WIDTH), F32), V((3, 2, 2, RB, WIDTH), F32), V((3, 2, 2, RB, WIDTH), F32),
            V((3, RB, WIDTH), F32),
            V((2, 4, 2, 32, 512), F32), V((2, 4, 2, 32, 512), F32), V((2, 4, 2, 32, 512), F32),
            V((2, 2, 32, 512), F32), V((2, 2, 2, 32, 512), F32),
            pltpu.SemaphoreType.DMA((3,)),
            pltpu.SemaphoreType.DMA((ncopies,)), pltpu.SemaphoreType.DMA((ncopies,)),
        ],
        compiler_params=pltpu.CompilerParams(
            collective_id=0, has_side_effects=True, vmem_limit_bytes=56 * 2**20
        ),
        cost_estimate=pl.CostEstimate(
            flops=6 * 2048 * 2048 * 256, bytes_accessed=5 * 2**20, transcendentals=2048 * 2048
        ),
        name="sinkhorn_adjoint",
    )(
        scale_x.reshape(32, L), adjoint_x.reshape(32, L),
        scale_y.reshape(8, L), adjoint_y.reshape(8, L),
        features_x.reshape(2, 16, 2, 64, WIDTH), features_y,
    )
    gx, gy = pl.pallas_call(
        finish, out_shape=shapes, in_specs=[vmem, vmem], out_specs=(vmem, vmem), name="finish",
    )(*parts)
    return gx, gy.T


def solution(mesh):
    in_specs = (P("row", None), P("row"), P("row"), P("col", None), P("col"), P("col"))
    out_specs = (P(("row", "col"), None), P("col", "row"))
    return jax.shard_map(body, mesh=mesh, in_specs=in_specs, out_specs=out_specs, check_vma=False)
```

```python
import functools
import math

import jax
import jax.numpy as jnp
from jax import lax
from jax.experimental import pallas as pl
from jax.experimental.pallas import tpu as pltpu
from jax.sharding import PartitionSpec as P

KERNEL_GAIN = 0.5
WIDTH = 256
FACTOR = KERNEL_GAIN / math.sqrt(WIDTH)
L = 128
F32 = jnp.float32
BF16 = jnp.bfloat16
MESH = pl.DeviceIdType.MESH
NX, NY, NZ = 4, 4, 8
STRIP = 256
HALF = 1024
RA = 40
RB = 64 - RA
OTHERS_Z = (4, 3, 5, 2, 6, 1, 7)
OTHERS_4 = (2, 1, 3)
RC = 24
GROUP_YC = tuple((a, c) for a in (2, 1, 3, 0) for c in (0, 1) if (a, c) != (0, 0))


def kernel(
    sx_ref, ax_ref, sy_ref, ay_ref, x_hbm, y_hbm, gx_ref, gy_ref,
    xf, yf, xb, yb, xt, plan, wts, syv, ayv, rowb, ub, rt, mx, axd, colacc,
    vrow, xrow, zsrc, zrow, vcol, crow, vcol2, crow2, avec, rtot, ctot,
    ga, gb, a1, a2, az, b1, bp, bm, bx, gy, gyo, gyc, y1, y2,
    in_sem, sem_s, sem_r,
):
    row = lax.axis_index("row")
    col = lax.axis_index("col")
    x = col // (NZ * 2)
    z = (col // 2) % NZ
    core = col % 2
    other = 1 - core

    def at(dy=0, dx=0, dz=0, dc=0):
        return (
            lax.rem(row + dy, NY),
            (lax.rem(x + dx, NX) * NZ + lax.rem(z + dz, NZ)) * 2 + lax.rem(core + dc, 2),
        )

    count = [0]
    sent = []

    def send(src, dst, device):
        n = count[0]
        count[0] += 1
        copy = pltpu.make_async_remote_copy(
            src_ref=src, dst_ref=dst, send_sem=sem_s.at[n], recv_sem=sem_r.at[n],
            device_id=device, device_id_type=MESH,
        )
        copy.start()
        sent.append(copy)
        return copy

    def drain():
        for copy in sent:
            copy.wait_send()
        sent.clear()

    loads = [
        pltpu.make_async_copy(y_hbm, yf.at[core], in_sem.at[0]),
        pltpu.make_async_copy(x_hbm.at[0, :, core], xf.at[:, 0], in_sem.at[1]),
        pltpu.make_async_copy(x_hbm.at[1, :, core], xf.at[:, 1], in_sem.at[2]),
    ]
    for copy in loads:
        copy.start()

    barrier = pltpu.get_barrier_semaphore()
    peers = (
        [at(dz=d) for d in OTHERS_Z] + [at(dx=d) for d in OTHERS_4]
        + [at(dy=a, dc=c) for a, c in GROUP_YC]
    )
    for peer in peers:
        pl.semaphore_signal(barrier, inc=1, device_id=peer, device_id_type=MESH)

    lane = lax.broadcasted_iota(jnp.int32, (16, L), 1)
    first = core == 0

    def mine(ref):
        low, high = ref[0:16, :], ref[16:32, :]
        low_r, high_r = pltpu.roll(low, 64, 1), pltpu.roll(high, 64, 1)
        return jnp.where(lane < 64, jnp.where(first, low, low_r), jnp.where(first, high_r, high))

    def spread(vec, dst, start):
        for m in range(vec.shape[0]):
            here = start + m * L
            dst[here:here + L, :] = jnp.broadcast_to(vec[m:m + 1, :], (L, L)).T

    def gather_rows(src, chunk, dst):
        for m in range(8):
            here = chunk * HALF + m * L
            dst[m:m + 1, :] = jnp.sum(src[here:here + L, :].T, axis=0, keepdims=True)

    axd[...] = mine(ax_ref)
    spread(mine(sx_ref), ub, 0)
    syv[core] = sy_ref[...]
    ayv[core] = ay_ref[...]
    for copy in loads:
        copy.wait()

    def cast_x(i, _):
        xb[pl.ds(i * L, 64), :] = xf[i, 0].astype(BF16)
        xb[pl.ds(i * L + 64, 64), :] = xf[i, 1].astype(BF16)
        return 0
    lax.fori_loop(0, 16, cast_x, 0)

    def cast_y(half):
        def step(i, _):
            yb[half, pl.ds(i * L, L), :] = yf[half, pl.ds(i * L, L), :].astype(BF16)
            return 0
        lax.fori_loop(0, 8, step, 0)
    cast_y(core)

    def fold8(v):
        return jnp.sum(v.reshape(-1, 8, L), axis=0)

    def make_plan(half, start, size, fresh):
        rows = slice(start, start + size)
        u = ub[rows, :]
        if fresh:
            acc_r = acc_m = None
        else:
            acc_r, acc_m = rt[rows, :], mx[rows, :]
        for j in range(4):
            s = lax.dot_general(
                xb[rows, :], yb[half, j * 256:(j + 1) * 256, :],
                (((1,), (1,)), ((), ())), preferred_element_type=F32,
            )
            for l in range(2):
                t = j * 2 + l
                p = (u * jnp.exp(s[:, l * L:(l + 1) * L] * FACTOR)) * syv[half, t:t + 1, :]
                plan[half, rows, t * L:(t + 1) * L] = p
                pa = p * ayv[half, t:t + 1, :]
                acc_r = p if acc_r is None else acc_r + p
                acc_m = pa if acc_m is None else acc_m + pa
                c = fold8(p)
                colacc[half, t] = c if start == 0 else colacc[half, t] + c
        rt[rows, :] = acc_r
        mx[rows, :] = acc_m

    sib = at(dc=1)
    make_plan(core, 0, 512, True)
    pl.semaphore_wait(barrier, len(peers))
    fetch = [
        send(y_hbm, yf.at[core], sib),
        send(sy_ref, syv.at[core], sib),
        send(ay_ref, ayv.at[core], sib),
    ]
    make_plan(core, 512, 1536, True)
    for copy in fetch:
        copy.wait_recv()
    cast_y(other)

    def rows_x(k, n, c):
        return [
            send(vrow.at[k, c, 0:n], xrow.at[k, c, q, 0:n], at(dx=d))
            for q, d in enumerate(OTHERS_4)
        ]

    def rows_z(k, n, c, copies):
        for copy in copies:
            copy.wait_recv()
        total = vrow[k, c, 0:n]
        for q in range(3):
            total = total + xrow[k, c, q, 0:n]
        zsrc[k, c, 0:n] = total
        return [
            send(zsrc.at[k, c, 0:n], zrow.at[k, c, q, 0:n], at(dz=d))
            for q, d in enumerate(OTHERS_Z)
        ]

    def rows_end(k, n, c, copies):
        for copy in copies:
            copy.wait_recv()
        total = zsrc[k, c, 0:n]
        for q in range(7):
            total = total + zrow[k, c, q, 0:n]
        return total

    in_x = []
    for c in range(2):
        make_plan(other, c * HALF, HALF, False)
        gather_rows(rt, c, vrow.at[0, c, 0])
        gather_rows(mx, c, vrow.at[0, c, 1])
        in_x.append(rows_x(0, 2, c))
    in_z = [rows_z(0, 2, c, in_x[c]) for c in range(2)]
    for half in range(2):
        for t in range(8):
            vcol[0, half * 8 + t:half * 8 + t + 1, :] = jnp.sum(
                colacc[half, t], axis=0, keepdims=True)

    def turn_x(i, _):
        rows = pl.ds(pl.multiple_of(i * L, L), L)
        xt[:, rows] = xb[rows, :].T
        return 0
    lax.fori_loop(0, 16, turn_x, 0)

    def back(c):
        for half in range(2):
            def strip(i, cols):
                rows = pl.ds(pl.multiple_of(c * HALF + i * STRIP, STRIP), STRIP)
                r = rowb[rows, :]
                return tuple(
                    cols[t] + fold8(plan[half, rows, t * L:(t + 1) * L] * r) for t in range(8)
                )
            init = tuple(jnp.zeros((8, L), F32) if c == 0 else colacc[half, t] for t in range(8))
            cols = lax.fori_loop(0, HALF // STRIP, strip, init)
            for t in range(8):
                colacc[half, t] = cols[t]

    def back_end(dst):
        for half in range(2):
            for t in range(8):
                dst[half * 8 + t:half * 8 + t + 1, :] = jnp.sum(
                    colacc[half, t], axis=0, keepdims=True)

    def sum_cols(src, dst):
        copies = [
            send(src, dst.at[q], at(dy=a, dc=c)) for q, (a, c) in enumerate(GROUP_YC)
        ]
        for copy in copies:
            copy.wait_recv()
        total = src[...]
        for q in range(7):
            total = total + dst[q]
        return total

    for c in range(2):
        total = rows_end(0, 2, c, in_z[c])
        rtot[c * 8:(c + 1) * 8, :] = total[0]
        spread(axd[c * 8:(c + 1) * 8, :] - total[1] / total[0], rowb, c * HALF)
        back(c)
    back_end(vcol.at[1])
    total = sum_cols(vcol, crow)
    ay_all = ayv[...].reshape(16, L)
    ctot[...] = total[0]
    avec[...] = ay_all - total[1] / total[0]

    in_x = []
    for c in range(2):
        def mix(i, _):
            rows = pl.ds(pl.multiple_of(c * HALF + i * STRIP, STRIP), STRIP)
            acc = jnp.zeros((STRIP, L), F32)
            for half in range(2):
                for t in range(8):
                    acc += plan[half, rows, t * L:(t + 1) * L] * avec[half * 8 + t:half * 8 + t + 1, :]
            mx[rows, :] = acc
            return 0
        lax.fori_loop(0, HALF // STRIP, mix, 0)
        gather_rows(mx, c, vrow.at[1, c, 0])
        in_x.append(rows_x(1, 1, c))
    in_z = [rows_z(1, 1, c, in_x[c]) for c in range(2)]
    for c in range(2):
        total = rows_end(1, 1, c, in_z[c])
        spread(axd[c * 8:(c + 1) * 8, :] - total[0] / rtot[c * 8:(c + 1) * 8, :], rowb, c * HALF)
        back(c)
    back_end(vcol2)
    avec[...] = ay_all - sum_cols(vcol2, crow2) / ctot[...]

    par = lax.rem(x, 2)

    def weigh(order):
        side = par if order == 0 else 1 - par
        rows = pl.ds(pl.multiple_of(side * HALF, HALF), HALF)
        r = rowb[rows, :]
        for half in range(2):
            for t in range(8):
                a = avec[half * 8 + t:half * 8 + t + 1, :]
                w = plan[half, rows, t * L:(t + 1) * L] * (r + a)
                wts[half, rows, t * L:(t + 1) * L] = w.astype(BF16)
        g = jnp.dot(wts[0, rows, :], yb[0], preferred_element_type=F32)
        g += jnp.dot(wts[1, rows, :], yb[1], preferred_element_type=F32)
        g = g * FACTOR
        for m in range(8):
            off = lax.rem(m + 8 - z, 8)
            pos = lax.rem(off + 6, 8)
            for h in range(2):
                xo = lax.rem(2 * h + side + 4 - x, 4)
                piece = g[m * L + h * 64:m * L + h * 64 + 64, :]
                ga[xo, pos] = piece[0:RA, :]
                gb[off, order, xo // 2] = piece[RA:64, :]

    right_x, left_x = at(dx=1), at(dx=3)
    right_z, left_z = at(dz=1), at(dz=7)
    right_y, left_y = at(dy=1), at(dy=3)

    def lo(c):
        return slice(4 * c, 4 * c + 2)

    def hi(c):
        return slice(4 * c + 2, 4 * c + 4)

    weigh(0)
    one_a = [None, None]
    two_a = [[], []]
    for c in range(2):
        one_a[c] = (
            send(ga.at[2, lo(c)], a1.at[c, 0], right_x), send(ga.at[2, hi(c)], a1.at[c, 1], left_x)
        )
    one_b = [send(gb.at[4, 0], b1.at[0], right_z), None]
    fwd = [[None, None], [None, None], [None, None]]
    bwd = [[None, None], [None, None], [None, None]]
    bwd[0][0] = send(gb.at[5, 0], bm.at[0, 0], left_z)
    weigh(1)

    def a_direct(c):
        two_a[c].append(send(ga.at[1, hi(c)], a2.at[0, hi(c)], right_x))
        two_a[c].append(send(ga.at[3, lo(c)], a2.at[1, lo(c)], left_x))

    def a_summed(c):
        one_a[c][0].wait_recv()
        ga[1, lo(c)] = ga[1, lo(c)] + a1[c, 0]
        two_a[c].append(send(ga.at[1, lo(c)], a2.at[0, lo(c)], right_x))
        one_a[c][1].wait_recv()
        ga[3, hi(c)] = ga[3, hi(c)] + a1[c, 1]
        two_a[c].append(send(ga.at[3, hi(c)], a2.at[1, hi(c)], left_x))

    up2, down2 = at(dz=2), at(dz=6)
    relay = []
    last_a = []

    def a_end(c):
        for copy in two_a[c]:
            copy.wait_recv()
        here = slice(4 * c, 4 * c + 4)
        ga[0, here] = ga[0, here] + a2[0, here] + a2[1, here]
        if c == 0:
            relay.append(send(ga.at[0, 2, 0:RC], az.at[0, 0:RC], up2))
            relay.append(send(ga.at[0, 2, RC:RA], az.at[0, RC:RA], down2))
            relay.append(send(ga.at[0, 1], az.at[1], right_z))
            relay.append(send(ga.at[0, 3], az.at[2], left_z))
        else:
            last_a.append(send(ga.at[0, 7], az.at[3], right_z))
            last_a.append(send(ga.at[0, 5], az.at[4], left_z))

    def a_relay():
        relay[0].wait_recv()
        relay[2].wait_recv()
        ga[0, 0, 0:RC] = ga[0, 0, 0:RC] + az[0, 0:RC] + az[1, 0:RC]
        ga[0, 0, RC:RA] = ga[0, 0, RC:RA] + az[1, RC:RA]
        last_a.append(send(ga.at[0, 0], az.at[5], up2))
        relay[1].wait_recv()
        relay[3].wait_recv()
        ga[0, 4, 0:RC] = ga[0, 4, 0:RC] + az[2, 0:RC]
        ga[0, 4, RC:RA] = ga[0, 4, RC:RA] + az[0, RC:RA] + az[2, RC:RA]
        last_a.append(send(ga.at[0, 4], az.at[6], down2))

    a_direct(0)
    one_b[1] = send(gb.at[4, 1], b1.at[1], left_z)
    fwd[0][1] = send(gb.at[3, 1], bp.at[0, 1], right_z)

    def cols_of(half, part, dst):
        g = jnp.dot(xt[...], wts[half, :, part * 512:(part + 1) * 512], preferred_element_type=F32)
        g = g * FACTOR
        for q in range(4):
            off = lax.rem(q + 4 - row, 4)
            for h in range(2):
                dst[part, off, h] = g[q * 64 + h * 32:q * 64 + h * 32 + 32, :]

    swap = []
    for part in range(2):
        cols_of(other, part, gyo)
        swap.append(send(gyo.at[part], gyc.at[part], sib))

    one_y = [None, None]
    two_y = [[], []]

    def y_start(part):
        cols_of(core, part, gy)
        swap[part].wait_recv()
        gy[part] = gy[part] + gyc[part]
        one_y[part] = (
            send(gy.at[part, 2, 0], y1.at[part, 0], right_y),
            send(gy.at[part, 2, 1], y1.at[part, 1], left_y),
        )

    def y_direct(part):
        two_y[part].append(send(gy.at[part, 1, 1], y2.at[0, part, 1], right_y))
        two_y[part].append(send(gy.at[part, 3, 0], y2.at[1, part, 0], left_y))

    def y_summed(part):
        one_y[part][0].wait_recv()
        gy[part, 1, 0] = gy[part, 1, 0] + y1[part, 0]
        two_y[part].append(send(gy.at[part, 1, 0], y2.at[0, part, 0], right_y))
        one_y[part][1].wait_recv()
        gy[part, 3, 1] = gy[part, 3, 1] + y1[part, 1]
        two_y[part].append(send(gy.at[part, 3, 1], y2.at[1, part, 1], left_y))

    def y_end(part):
        for copy in two_y[part]:
            copy.wait_recv()
        for h in range(2):
            gy_ref[h * 32:(h + 1) * 32, part * 512:(part + 1) * 512] = (
                gy[part, 0, h] + y2[0, part, h] + y2[1, part, h]
            )

    def z_fwd(s, p):
        fwd[s - 3][p].wait_recv()
        gb[5 - s, p] = gb[5 - s, p] + bp[s - 3, p]
        fwd[s - 2][p] = send(gb.at[5 - s, p], bp.at[s - 2, p], right_z)

    def z_bwd(s, p):
        bwd[s - 3][p].wait_recv()
        gb[3 + s, p] = gb[3 + s, p] + bm[s - 3, p]
        bwd[s - 2][p] = send(gb.at[3 + s, p], bm.at[s - 2, p], left_z)

    last_b = []

    def b_end(p):
        fwd[2][p].wait_recv()
        bwd[2][p].wait_recv()
        gb[0, p] = gb[0, p] + bp[2, p] + bm[2, p]
        for h in range(2):
            if (h, p) != (0, 0):
                last_b.append(send(gb.at[0, p, h], bx.at[len(last_b)], at(dx=2 * h + p)))

    one_b[0].wait_recv()
    gb[3, 0] = gb[3, 0] + b1[0]
    fwd[0][0] = send(gb.at[3, 0], bp.at[0, 0], right_z)
    z_bwd(3, 0)
    a_summed(0)
    a_direct(1)
    z_fwd(3, 1)
    one_b[1].wait_recv()
    gb[5, 1] = gb[5, 1] + b1[1]
    bwd[0][1] = send(gb.at[5, 1], bm.at[0, 1], left_z)
    a_summed(1)
    y_start(0)
    z_fwd(3, 0)
    z_bwd(4, 0)
    y_start(1)
    y_direct(0)
    y_direct(1)
    z_fwd(4, 1)
    z_bwd(3, 1)
    a_end(0)
    z_fwd(4, 0)
    y_summed(0)
    z_bwd(4, 1)
    a_end(1)
    y_summed(1)
    a_relay()
    b_end(0)
    b_end(1)
    y_end(0)
    y_end(1)
    total = ga[0, 6]
    for q in range(4):
        last_a[q].wait_recv()
        total = total + az[3 + q]
    gx_ref[0:RA, :] = total
    total = gb[0, 0, 0]
    for q in range(3):
        last_b[q].wait_recv()
        total = total + bx[q]
    gx_ref[RA:64, :] = total
    assert count[0] == sem_s.shape[0]
    drain()


def finish(a_ref, b_ref, gx_ref, gy_ref):
    gx_ref[...] = a_ref[...]
    gy_ref[...] = b_ref[...]


def body(features_x, scale_x, adjoint_x, features_y, scale_y, adjoint_y):
    vmem = pl.BlockSpec(memory_space=pltpu.VMEM)
    anym = pl.BlockSpec(memory_space=pl.ANY)
    V = pltpu.VMEM
    ncopies = 108
    shapes = (
        jax.ShapeDtypeStruct((64, WIDTH), F32),
        jax.ShapeDtypeStruct((64, 1024), F32),
    )
    parts = pl.pallas_call(
        kernel,
        out_shape=shapes,
        in_specs=[vmem, vmem, vmem, vmem, anym, anym],
        out_specs=(vmem, vmem),
        scratch_shapes=[
            V((16, 2, 64, WIDTH), F32), V((2, 1024, WIDTH), F32),
            V((2048, WIDTH), BF16), V((2, 1024, WIDTH), BF16), V((WIDTH, 2048), BF16),
            V((2, 2048, 1024), F32), V((2, 2048, 1024), BF16),
            V((2, 8, L), F32), V((2, 8, L), F32),
            V((2048, L), F32), V((2048, L), F32), V((2048, L), F32), V((2048, L), F32),
            V((16, L), F32), V((2, 8, 8, L), F32),
            V((2, 2, 2, 8, L), F32), V((2, 2, 3, 2, 8, L), F32),
            V((2, 2, 2, 8, L), F32), V((2, 2, 7, 2, 8, L), F32),
            V((2, 16, L), F32), V((7, 2, 16, L), F32),
            V((16, L), F32), V((7, 16, L), F32), V((16, L), F32), V((16, L), F32), V((16, L), F32),
            V((4, 8, RA, WIDTH), F32), V((8, 2, 2, RB, WIDTH), F32),
            V((2, 2, 2, RA, WIDTH), F32), V((2, 8, RA, WIDTH), F32), V((7, RA, WIDTH), F32),
            V((2, 2, RB, WIDTH), F32), V((3, 2, 2, RB, WIDTH), F32), V((3, 2, 2, RB, WIDTH), F32),
            V((3, RB, WIDTH), F32),
            V((2, 4, 2, 32, 512), F32), V((2, 4, 2, 32, 512), F32), V((2, 4, 2, 32, 512), F32),
            V((2, 2, 32, 512), F32), V((2, 2, 2, 32, 512), F32),
            pltpu.SemaphoreType.DMA((3,)),
            pltpu.SemaphoreType.DMA((ncopies,)), pltpu.SemaphoreType.DMA((ncopies,)),
        ],
        compiler_params=pltpu.CompilerParams(
            collective_id=0, has_side_effects=True, vmem_limit_bytes=56 * 2**20
        ),
        cost_estimate=pl.CostEstimate(
            flops=6 * 2048 * 2048 * 256, bytes_accessed=5 * 2**20, transcendentals=2048 * 2048
        ),
        name="sinkhorn_adjoint",
    )(
        scale_x.reshape(32, L), adjoint_x.reshape(32, L),
        scale_y.reshape(8, L), adjoint_y.reshape(8, L),
        features_x.reshape(2, 16, 2, 64, WIDTH), features_y,
    )
    gx, gy = pl.pallas_call(
        finish, out_shape=shapes, in_specs=[vmem, vmem], out_specs=(vmem, vmem), name="finish",
    )(*parts)
    return gx, gy.T


def solution(mesh):
    in_specs = (P("row", None), P("row"), P("row"), P("col", None), P("col"), P("col"))
    out_specs = (P(("row", "col"), None), P("col", "row"))
    return jax.shard_map(body, mesh=mesh, in_specs=in_specs, out_specs=out_specs, check_vma=False)
```

```python
import functools
import math

import jax
import jax.numpy as jnp
from jax import lax
from jax.experimental import pallas as pl
from jax.experimental.pallas import tpu as pltpu
from jax.sharding import PartitionSpec as P

KERNEL_GAIN = 0.5
WIDTH = 256
FACTOR = KERNEL_GAIN / math.sqrt(WIDTH)
FACTOR2 = FACTOR / math.log(2.0)
L = 128
F32 = jnp.float32
BF16 = jnp.bfloat16
MESH = pl.DeviceIdType.MESH
NX, NY, NZ = 4, 4, 8
STRIP = 256
HALF = 1024
RA = 40
RB = 64 - RA
OTHERS_Z = (4, 3, 5, 2, 6, 1, 7)
OTHERS_4 = (2, 1, 3)
RC = 24
GROUP_YC = tuple((a, c) for a in (2, 1, 3, 0) for c in (0, 1) if (a, c) != (0, 0))


def kernel(
    sx_ref, ax_ref, sy_ref, ay_ref, x_hbm, y_hbm, gx_ref, gy_ref,
    xf, yf, xb, yb, xt, plan, wts, syv, ayv, rowb, ub, rt, mx, axd, colacc,
    vrow, xrow, zsrc, zrow, vcol, crow, avec, rtot, ctot,
    ga, gb, a1, a2, az, b1, bp, bm, bx, gy, gyo, gyc, y1, y2,
    in_sem, sem_s, sem_r,
):
    row = lax.axis_index("row")
    col = lax.axis_index("col")
    x = col // (NZ * 2)
    z = (col // 2) % NZ
    core = col % 2
    other = 1 - core

    def at(dy=0, dx=0, dz=0, dc=0):
        return (
            lax.rem(row + dy, NY),
            (lax.rem(x + dx, NX) * NZ + lax.rem(z + dz, NZ)) * 2 + lax.rem(core + dc, 2),
        )

    count = [0]
    sent = []

    def send(src, dst, device):
        n = count[0]
        count[0] += 1
        copy = pltpu.make_async_remote_copy(
            src_ref=src, dst_ref=dst, send_sem=sem_s.at[n], recv_sem=sem_r.at[n],
            device_id=device, device_id_type=MESH,
        )
        copy.start()
        sent.append(copy)
        return copy

    def drain():
        for copy in sent:
            copy.wait_send()
        sent.clear()

    loads = [
        pltpu.make_async_copy(y_hbm, yf.at[core], in_sem.at[0]),
        pltpu.make_async_copy(x_hbm.at[0, 0:4, core], xf.at[0:4, 0], in_sem.at[1]),
        pltpu.make_async_copy(x_hbm.at[1, 0:4, core], xf.at[0:4, 1], in_sem.at[2]),
        pltpu.make_async_copy(x_hbm.at[0, 4:16, core], xf.at[4:16, 0], in_sem.at[3]),
        pltpu.make_async_copy(x_hbm.at[1, 4:16, core], xf.at[4:16, 1], in_sem.at[4]),
    ]
    for copy in loads:
        copy.start()

    barrier = pltpu.get_barrier_semaphore()
    peers = (
        [at(dz=d) for d in OTHERS_Z] + [at(dx=d) for d in OTHERS_4]
        + [at(dy=a, dc=c) for a, c in GROUP_YC]
    )
    for peer in peers:
        pl.semaphore_signal(barrier, inc=1, device_id=peer, device_id_type=MESH)

    lane = lax.broadcasted_iota(jnp.int32, (16, L), 1)
    first = core == 0

    def mine(ref):
        low, high = ref[0:16, :], ref[16:32, :]
        low_r, high_r = pltpu.roll(low, 64, 1), pltpu.roll(high, 64, 1)
        return jnp.where(lane < 64, jnp.where(first, low, low_r), jnp.where(first, high_r, high))

    def spread(vec, dst, start):
        for m in range(vec.shape[0]):
            here = start + m * L
            dst[here:here + L, :] = jnp.broadcast_to(vec[m:m + 1, :], (L, L)).T

    def gather_rows(src, chunk, dst):
        for m in range(8):
            here = chunk * HALF + m * L
            dst[m:m + 1, :] = jnp.sum(src[here:here + L, :].T, axis=0, keepdims=True)

    axd[...] = mine(ax_ref)
    spread(jnp.log2(mine(sx_ref)), ub, 0)
    syv[core] = sy_ref[...]
    ayv[core] = ay_ref[...]
    for copy in loads[0:3]:
        copy.wait()

    def cast_x(i, _):
        xb[pl.ds(i * L, 64), :] = xf[i, 0].astype(BF16)
        xb[pl.ds(i * L + 64, 64), :] = xf[i, 1].astype(BF16)
        return 0
    lax.fori_loop(0, 4, cast_x, 0)

    def cast_y(half):
        def step(i, _):
            yb[half, pl.ds(i * L, L), :] = yf[half, pl.ds(i * L, L), :].astype(BF16)
            return 0
        lax.fori_loop(0, 8, step, 0)
    cast_y(core)

    def fold8(v):
        return jnp.sum(v.reshape(-1, 8, L), axis=0)

    def make_plan(half, start, size, fresh):
        rows = slice(start, start + size)
        u = ub[rows, :]
        if fresh:
            acc_r = acc_m = None
        else:
            acc_r, acc_m = rt[rows, :], mx[rows, :]
        for j in range(4):
            s = lax.dot_general(
                xb[rows, :], yb[half, j * 256:(j + 1) * 256, :],
                (((1,), (1,)), ((), ())), preferred_element_type=F32,
            )
            for l in range(2):
                t = j * 2 + l
                p = jnp.exp2(s[:, l * L:(l + 1) * L] * FACTOR2 + u) * syv[half, t:t + 1, :]
                plan[half, rows, t * L:(t + 1) * L] = p
                pa = p * ayv[half, t:t + 1, :]
                acc_r = p if acc_r is None else acc_r + p
                acc_m = pa if acc_m is None else acc_m + pa
                c = fold8(p)
                colacc[half, t] = c if start == 0 else colacc[half, t] + c
        rt[rows, :] = acc_r
        mx[rows, :] = acc_m

    sib = at(dc=1)
    make_plan(core, 0, 512, True)
    pl.semaphore_wait(barrier, len(peers))
    fetch = [
        send(y_hbm, yf.at[core], sib),
        send(sy_ref, syv.at[core], sib),
        send(ay_ref, ayv.at[core], sib),
    ]
    for copy in loads[3:]:
        copy.wait()
    lax.fori_loop(4, 16, cast_x, 0)
    make_plan(core, 512, 1536, True)
    for copy in fetch:
        copy.wait_recv()
    cast_y(other)

    def rows_x(k, n, c):
        return [
            send(vrow.at[k, c, 0:n], xrow.at[k, c, q, 0:n], at(dx=d))
            for q, d in enumerate(OTHERS_4)
        ]

    def rows_z(k, n, c, copies):
        for copy in copies:
            copy.wait_recv()
        total = vrow[k, c, 0:n]
        for q in range(3):
            total = total + xrow[k, c, q, 0:n]
        zsrc[k, c, 0:n] = total
        return [
            send(zsrc.at[k, c, 0:n], zrow.at[k, c, q, 0:n], at(dz=d))
            for q, d in enumerate(OTHERS_Z)
        ]

    def rows_end(k, n, c, copies):
        for copy in copies:
            copy.wait_recv()
        total = zsrc[k, c, 0:n]
        for q in range(7):
            total = total + zrow[k, c, q, 0:n]
        return total

    in_x = []
    for c in range(2):
        make_plan(other, c * HALF, HALF, False)
        gather_rows(rt, c, vrow.at[0, c, 0])
        gather_rows(mx, c, vrow.at[0, c, 1])
        in_x.append(rows_x(0, 2, c))
    def back_end(dst):
        for half in range(2):
            for t in range(8):
                dst[half * 8 + t:half * 8 + t + 1, :] = jnp.sum(
                    colacc[half, t], axis=0, keepdims=True)

    def cols_start(k):
        return [
            send(vcol.at[k], crow.at[k, q], at(dy=a, dc=c)) for q, (a, c) in enumerate(GROUP_YC)
        ]

    def cols_end(k, copies):
        for copy in copies:
            copy.wait_recv()
        total = vcol[k]
        for q in range(7):
            total = total + crow[k, q]
        return total

    in_z = [rows_z(0, 2, c, in_x[c]) for c in range(2)]
    back_end(vcol.at[0])
    in_col = cols_start(0)

    def turn_x(i, _):
        rows = pl.ds(pl.multiple_of(i * L, L), L)
        xt[:, rows] = xb[rows, :].T
        return 0
    lax.fori_loop(0, 16, turn_x, 0)

    def back(c):
        for half in range(2):
            def strip(i, cols):
                rows = pl.ds(pl.multiple_of(c * HALF + i * STRIP, STRIP), STRIP)
                r = rowb[rows, :]
                return tuple(
                    cols[t] + fold8(plan[half, rows, t * L:(t + 1) * L] * r) for t in range(8)
                )
            init = tuple(jnp.zeros((8, L), F32) if c == 0 else colacc[half, t] for t in range(8))
            cols = lax.fori_loop(0, HALF // STRIP, strip, init)
            for t in range(8):
                colacc[half, t] = cols[t]

    for c in range(2):
        total = rows_end(0, 2, c, in_z[c])
        rtot[c * 8:(c + 1) * 8, :] = total[0]
        spread(axd[c * 8:(c + 1) * 8, :] - total[1] / total[0], rowb, c * HALF)
        back(c)
    back_end(vcol.at[1])
    more = cols_start(1)
    ay_all = ayv[...].reshape(16, L)
    col_tot = cols_end(0, in_col)
    ctot[...] = col_tot
    avec[...] = ay_all - cols_end(1, more) / col_tot

    in_x = []
    for c in range(2):
        def mix(i, _):
            rows = pl.ds(pl.multiple_of(c * HALF + i * STRIP, STRIP), STRIP)
            acc = jnp.zeros((STRIP, L), F32)
            for half in range(2):
                for t in range(8):
                    acc += plan[half, rows, t * L:(t + 1) * L] * avec[half * 8 + t:half * 8 + t + 1, :]
            mx[rows, :] = acc
            return 0
        lax.fori_loop(0, HALF // STRIP, mix, 0)
        gather_rows(mx, c, vrow.at[1, c, 0])
        in_x.append(rows_x(1, 1, c))
    in_z = [rows_z(1, 1, c, in_x[c]) for c in range(2)]
    for c in range(2):
        total = rows_end(1, 1, c, in_z[c])
        spread(axd[c * 8:(c + 1) * 8, :] - total[0] / rtot[c * 8:(c + 1) * 8, :], rowb, c * HALF)
        back(c)
    back_end(vcol.at[2])
    avec[...] = ay_all - cols_end(2, cols_start(2)) / ctot[...]

    par = lax.rem(x, 2)

    def weigh(order):
        side = par if order == 0 else 1 - par
        rows = pl.ds(pl.multiple_of(side * HALF, HALF), HALF)
        r = rowb[rows, :]
        for half in range(2):
            for t in range(8):
                a = avec[half * 8 + t:half * 8 + t + 1, :]
                w = plan[half, rows, t * L:(t + 1) * L] * (r + a)
                wts[half, rows, t * L:(t + 1) * L] = w.astype(BF16)
        g = jnp.dot(wts[0, rows, :], yb[0], preferred_element_type=F32)
        g += jnp.dot(wts[1, rows, :], yb[1], preferred_element_type=F32)
        g = g * FACTOR
        for m in range(8):
            off = lax.rem(m + 8 - z, 8)
            pos = lax.rem(off + 6, 8)
            for h in range(2):
                xo = lax.rem(2 * h + side + 4 - x, 4)
                piece = g[m * L + h * 64:m * L + h * 64 + 64, :]
                ga[xo, pos] = piece[0:RA, :]
                gb[off, order, xo // 2] = piece[RA:64, :]

    right_x, left_x = at(dx=1), at(dx=3)
    right_z, left_z = at(dz=1), at(dz=7)
    right_y, left_y = at(dy=1), at(dy=3)

    def lo(c):
        return slice(4 * c, 4 * c + 2)

    def hi(c):
        return slice(4 * c + 2, 4 * c + 4)

    weigh(0)
    one_a = [None, None]
    two_a = [[], []]
    for c in range(2):
        one_a[c] = (
            send(ga.at[2, lo(c)], a1.at[c, 0], right_x), send(ga.at[2, hi(c)], a1.at[c, 1], left_x)
        )
    one_b = [send(gb.at[4, 0], b1.at[0], right_z), None]
    fwd = [[None, None], [None, None], [None, None]]
    bwd = [[None, None], [None, None], [None, None]]
    bwd[0][0] = send(gb.at[5, 0], bm.at[0, 0], left_z)
    weigh(1)

    def a_direct(c):
        two_a[c].append(send(ga.at[1, hi(c)], a2.at[0, hi(c)], right_x))
        two_a[c].append(send(ga.at[3, lo(c)], a2.at[1, lo(c)], left_x))

    def a_summed(c):
        one_a[c][0].wait_recv()
        ga[1, lo(c)] = ga[1, lo(c)] + a1[c, 0]
        two_a[c].append(send(ga.at[1, lo(c)], a2.at[0, lo(c)], right_x))
        one_a[c][1].wait_recv()
        ga[3, hi(c)] = ga[3, hi(c)] + a1[c, 1]
        two_a[c].append(send(ga.at[3, hi(c)], a2.at[1, hi(c)], left_x))

    up2, down2 = at(dz=2), at(dz=6)
    relay = []
    last_a = []

    def a_end(c):
        for copy in two_a[c]:
            copy.wait_recv()
        here = slice(4 * c, 4 * c + 4)
        ga[0, here] = ga[0, here] + a2[0, here] + a2[1, here]
        if c == 0:
            relay.append(send(ga.at[0, 2, 0:RC], az.at[0, 0:RC], up2))
            relay.append(send(ga.at[0, 2, RC:RA], az.at[0, RC:RA], down2))
            relay.append(send(ga.at[0, 1], az.at[1], right_z))
            relay.append(send(ga.at[0, 3], az.at[2], left_z))
        else:
            last_a.append(send(ga.at[0, 7], az.at[3], right_z))
            last_a.append(send(ga.at[0, 5], az.at[4], left_z))

    def a_relay():
        relay[0].wait_recv()
        relay[2].wait_recv()
        ga[0, 0, 0:RC] = ga[0, 0, 0:RC] + az[0, 0:RC] + az[1, 0:RC]
        ga[0, 0, RC:RA] = ga[0, 0, RC:RA] + az[1, RC:RA]
        last_a.append(send(ga.at[0, 0], az.at[5], up2))
        relay[1].wait_recv()
        relay[3].wait_recv()
        ga[0, 4, 0:RC] = ga[0, 4, 0:RC] + az[2, 0:RC]
        ga[0, 4, RC:RA] = ga[0, 4, RC:RA] + az[0, RC:RA] + az[2, RC:RA]
        last_a.append(send(ga.at[0, 4], az.at[6], down2))

    a_direct(0)
    one_b[1] = send(gb.at[4, 1], b1.at[1], left_z)
    fwd[0][1] = send(gb.at[3, 1], bp.at[0, 1], right_z)

    def cols_of(half, part, dst):
        g = jnp.dot(xt[...], wts[half, :, part * 512:(part + 1) * 512], preferred_element_type=F32)
        g = g * FACTOR
        for q in range(4):
            off = lax.rem(q + 4 - row, 4)
            for h in range(2):
                dst[part, off, h] = g[q * 64 + h * 32:q * 64 + h * 32 + 32, :]

    swap = []
    for part in range(2):
        cols_of(other, part, gyo)
        swap.append(send(gyo.at[part], gyc.at[part], sib))

    one_y = [None, None]
    two_y = [[], []]

    def y_start(part):
        cols_of(core, part, gy)
        swap[part].wait_recv()
        gy[part] = gy[part] + gyc[part]
        one_y[part] = (
            send(gy.at[part, 2, 0], y1.at[part, 0], right_y),
            send(gy.at[part, 2, 1], y1.at[part, 1], left_y),
        )

    def y_direct(part):
        two_y[part].append(send(gy.at[part, 1, 1], y2.at[0, part, 1], right_y))
        two_y[part].append(send(gy.at[part, 3, 0], y2.at[1, part, 0], left_y))

    def y_summed(part):
        one_y[part][0].wait_recv()
        gy[part, 1, 0] = gy[part, 1, 0] + y1[part, 0]
        two_y[part].append(send(gy.at[part, 1, 0], y2.at[0, part, 0], right_y))
        one_y[part][1].wait_recv()
        gy[part, 3, 1] = gy[part, 3, 1] + y1[part, 1]
        two_y[part].append(send(gy.at[part, 3, 1], y2.at[1, part, 1], left_y))

    def y_end(part):
        for copy in two_y[part]:
            copy.wait_recv()
        for h in range(2):
            gy_ref[h * 32:(h + 1) * 32, part * 512:(part + 1) * 512] = (
                gy[part, 0, h] + y2[0, part, h] + y2[1, part, h]
            )

    def z_fwd(s, p):
        fwd[s - 3][p].wait_recv()
        gb[5 - s, p] = gb[5 - s, p] + bp[s - 3, p]
        fwd[s - 2][p] = send(gb.at[5 - s, p], bp.at[s - 2, p], right_z)

    def z_bwd(s, p):
        bwd[s - 3][p].wait_recv()
        gb[3 + s, p] = gb[3 + s, p] + bm[s - 3, p]
        bwd[s - 2][p] = send(gb.at[3 + s, p], bm.at[s - 2, p], left_z)

    last_b = []

    def b_end(p):
        fwd[2][p].wait_recv()
        bwd[2][p].wait_recv()
        gb[0, p] = gb[0, p] + bp[2, p] + bm[2, p]
        for h in range(2):
            if (h, p) != (0, 0):
                last_b.append(send(gb.at[0, p, h], bx.at[len(last_b)], at(dx=2 * h + p)))

    one_b[0].wait_recv()
    gb[3, 0] = gb[3, 0] + b1[0]
    fwd[0][0] = send(gb.at[3, 0], bp.at[0, 0], right_z)
    z_bwd(3, 0)
    a_summed(0)
    a_direct(1)
    z_fwd(3, 1)
    one_b[1].wait_recv()
    gb[5, 1] = gb[5, 1] + b1[1]
    bwd[0][1] = send(gb.at[5, 1], bm.at[0, 1], left_z)
    a_summed(1)
    y_start(0)
    z_fwd(3, 0)
    z_bwd(4, 0)
    y_start(1)
    y_direct(0)
    y_direct(1)
    z_fwd(4, 1)
    z_bwd(3, 1)
    a_end(0)
    z_fwd(4, 0)
    y_summed(0)
    z_bwd(4, 1)
    a_end(1)
    y_summed(1)
    a_relay()
    b_end(0)
    b_end(1)
    y_end(0)
    y_end(1)
    total = ga[0, 6]
    for q in range(4):
        last_a[q].wait_recv()
        total = total + az[3 + q]
    gx_ref[0:RA, :] = total
    total = gb[0, 0, 0]
    for q in range(3):
        last_b[q].wait_recv()
        total = total + bx[q]
    gx_ref[RA:64, :] = total
    assert count[0] == sem_s.shape[0]
    drain()


def body(features_x, scale_x, adjoint_x, features_y, scale_y, adjoint_y):
    vmem = pl.BlockSpec(memory_space=pltpu.VMEM)
    anym = pl.BlockSpec(memory_space=pl.ANY)
    V = pltpu.VMEM
    ncopies = 115
    gx, gy = pl.pallas_call(
        kernel,
        out_shape=(V((64, WIDTH), F32), V((64, 1024), F32)),
        in_specs=[vmem, vmem, vmem, vmem, anym, anym],
        out_specs=(vmem, vmem),
        scratch_shapes=[
            V((16, 2, 64, WIDTH), F32), V((2, 1024, WIDTH), F32),
            V((2048, WIDTH), BF16), V((2, 1024, WIDTH), BF16), V((WIDTH, 2048), BF16),
            V((2, 2048, 1024), F32), V((2, 2048, 1024), BF16),
            V((2, 8, L), F32), V((2, 8, L), F32),
            V((2048, L), F32), V((2048, L), F32), V((2048, L), F32), V((2048, L), F32),
            V((16, L), F32), V((2, 8, 8, L), F32),
            V((2, 2, 2, 8, L), F32), V((2, 2, 3, 2, 8, L), F32),
            V((2, 2, 2, 8, L), F32), V((2, 2, 7, 2, 8, L), F32),
            V((3, 16, L), F32), V((3, 7, 16, L), F32),
            V((16, L), F32), V((16, L), F32), V((16, L), F32),
            V((4, 8, RA, WIDTH), F32), V((8, 2, 2, RB, WIDTH), F32),
            V((2, 2, 2, RA, WIDTH), F32), V((2, 8, RA, WIDTH), F32), V((7, RA, WIDTH), F32),
            V((2, 2, RB, WIDTH), F32), V((3, 2, 2, RB, WIDTH), F32), V((3, 2, 2, RB, WIDTH), F32),
            V((3, RB, WIDTH), F32),
            V((2, 4, 2, 32, 512), F32), V((2, 4, 2, 32, 512), F32), V((2, 4, 2, 32, 512), F32),
            V((2, 2, 32, 512), F32), V((2, 2, 2, 32, 512), F32),
            pltpu.SemaphoreType.DMA((5,)),
            pltpu.SemaphoreType.DMA((ncopies,)), pltpu.SemaphoreType.DMA((ncopies,)),
        ],
        compiler_params=pltpu.CompilerParams(
            collective_id=0, has_side_effects=True, vmem_limit_bytes=56 * 2**20
        ),
        cost_estimate=pl.CostEstimate(
            flops=6 * 2048 * 2048 * 256, bytes_accessed=5 * 2**20, transcendentals=2048 * 2048
        ),
        name="sinkhorn_adjoint",
    )(
        scale_x.reshape(32, L), adjoint_x.reshape(32, L),
        scale_y.reshape(8, L), adjoint_y.reshape(8, L),
        features_x.reshape(2, 16, 2, 64, WIDTH), features_y,
    )
    return gx, gy.T


def solution(mesh):
    in_specs = (P("row", None), P("row"), P("row"), P("col", None), P("col"), P("col"))
    out_specs = (P(("row", "col"), None), P("col", "row"))
    return jax.shard_map(body, mesh=mesh, in_specs=in_specs, out_specs=out_specs, check_vma=False)
```
